32 devices in a mesh: seq: 8 (over y, x, core), head: 4 (over z).
Axes of the slice: x: 2, y: 2, z: 4, core: 2. Of those that a mesh axis runs over, the one named last changes fastest.
Arguments:
- inputs: bfloat16 [8192, 5376], P(('seq', 'head')), may hold values from -18 to 18
- queries: bfloat16 [8192, 2048], P('seq', 'head'), may hold values from -12 to 12
- key_rows: bfloat16 [8192, 1024], P('seq', 'head'), may hold values from -12 to 12
- values: bfloat16 [8192, 1024], P('seq', 'head'), may hold values from -6 to 6
- out_grad: bfloat16 [8192, 2048], P('seq', 'head'), may hold values from -6 to 6
- band_start: int32 [8192], P('seq'), may hold values from 0 to 8191, as said below
- owners: int32 [4, 6], replicated, may hold values from 0 to 7, as said below
Outputs:
- left_stat: float32 [8, 4, 1024, 1024], P('seq', 'head')
- right_stat: float32 [8, 4, 1024, 1024], P('seq', 'head')
The draws below stay inside these ranges and needn't reach their ends.
Inputs may be any that keep to these rules, and one draw needn't show every extreme that they name: band_start[i] lies between i - 1023 and i, and never decreases with i. `owners`: the 6 entries of a row differ.
All inputs are finite; a program needn't handle non-finite values.
Results may differ from the reference program's by a relative error of at most 0.015.
Values may be sent and summed in bfloat16 or wider, within the bound.
A program may use at most 128 MiB of HBM per device.

```python
import jax
import jax.numpy as jnp
from jax import lax

D = 5376
HD = 128
KV_DEV = 2
QPK = 2
WINDOW = 1024
BLOCK = 1024
TOK_DEV = 1024
TOKENS = 8192
KVH = 8
QH = 16
CPD = 1024
NBLK = 6
N_SEQ = 8
N_HEAD = 4


def drawn_parts(key):
    base_keys = jnp.clip(jax.random.normal(jax.random.fold_in(key, 11), (TOKENS, KVH, HD), jnp.float32), -6.0, 6.0)
    base_queries = jnp.clip(jax.random.normal(jax.random.fold_in(key, 12), (TOKENS, KVH, QPK, HD), jnp.float32), -6.0, 6.0)
    base_queries = jnp.clip(base_queries, -12.0, 12.0).reshape(TOKENS, QH * HD)
    base_keys = jnp.clip(base_keys, -12.0, 12.0).reshape(TOKENS, KVH * HD)
    return (base_queries, base_keys)


def draw_queries(key, part):
    return drawn_parts(key)[0].astype(jnp.bfloat16)


def draw_key_rows(key, part):
    return drawn_parts(key)[1].astype(jnp.bfloat16)


def draw_inputs(key, part):
    position_scale = 1.0 + 2.0 * jnp.arange(TOKENS, dtype=jnp.float32) / (TOKENS - 1)
    base_rows = jnp.clip(jax.random.normal(jax.random.fold_in(key, 22), (TOKENS, D), jnp.float32), -6.0, 6.0)
    return (base_rows * position_scale[:, None]).astype(jnp.bfloat16)


def draw_band_start(key, part):
    index_rows = jnp.arange(TOKENS, dtype=jnp.int32)
    coin_marks = jax.random.randint(key, (TOKENS,), 0, 4 * WINDOW)
    starts = (coin_marks == 0) | (index_rows == 0) | (index_rows == TOKENS - 1)
    doc_first = lax.cummax(jnp.where(starts, index_rows, 0), axis=0)
    return jnp.maximum(index_rows - WINDOW + 1, doc_first).astype(jnp.int32)


def draw_owners(key, part):

    def one_row(current_row_index):
        token_permutation_order = jax.random.permutation(jax.random.fold_in(key, current_row_index), N_SEQ).astype(jnp.int32)
        slot_ids = jnp.arange(N_SEQ, dtype=jnp.int32)
        document_end_flags = (slot_ids == 0) | (slot_ids == N_SEQ - 1)
        extra_score_bias = jnp.where((current_row_index == 0) & document_end_flags, N_SEQ, 0).astype(jnp.int32)
        attention_logits = token_permutation_order + extra_score_bias
        chosen = lax.top_k(attention_logits, NBLK)[1]
        return chosen.astype(jnp.int32)
    return jax.vmap(one_row)(jnp.arange(N_HEAD, dtype=jnp.int32))


def block_scale(own_key, dims, shards, low, high):
    def one(axis_at, shards_of):
        draws = jax.random.uniform(jax.random.fold_in(jax.random.fold_in(own_key, 6), axis_at), (shards_of,), jnp.float32, low / len(shards), high / len(shards))
        return jnp.repeat(jnp.exp(draws), dims[axis_at] // shards_of).reshape((-1,) + (1,) * (len(dims) - axis_at - 1))

    level = one(*shards[0])
    for cut in shards[1:]:
        level = level * one(*cut)
    return level


def gaussian(own_key, shape, scale, reach, shards=(), held_as=jnp.bfloat16):
    array = jax.random.normal(own_key, shape, jnp.float32) * scale
    if len(shards) > 0:
        array = block_scale(own_key, shape, shards, -0.22, 0.18) * array
    return jnp.clip(array, min=-reach, max=reach).astype(held_as)


def setup_inputs(seed: int = 0) -> dict:
    keys = jax.random.split(jax.random.key(seed), 8)
    return {
        "inputs": draw_inputs(jax.random.fold_in(keys[7], 71), 0),
        "queries": draw_queries(jax.random.fold_in(keys[7], 71), 0),
        "key_rows": draw_key_rows(jax.random.fold_in(keys[7], 71), 0),
        "values": gaussian(keys[3], (TOKENS, KVH * HD), 1.0, 6.0, ((0, 8), (1, 4))),
        "out_grad": gaussian(keys[4], (TOKENS, QH * HD), 1.0, 6.0, ((0, 8), (1, 4))),
        "band_start": draw_band_start(jax.random.fold_in(keys[7], 71), 0),
        "owners": draw_owners(jax.random.fold_in(keys[7], 71), 0),
    }


score_scale = 168.0 ** -0.5
rotary_frequency_base = 10000.0
neg_large = -1e30
top_precision = lax.Precision.HIGHEST


def rope_tables(positions, head_size):
    half_size = head_size // 2
    frequency = jnp.power(rotary_frequency_base, -2.0 * jnp.arange(half_size, dtype=jnp.float32) / head_size)
    angles = positions.astype(jnp.float32)[:, None] * frequency[None, :]
    cosine_table = jnp.concatenate([jnp.cos(angles), jnp.cos(angles)], 1)
    sine_table = jnp.concatenate([jnp.sin(angles), jnp.sin(angles)], 1)
    return cosine_table, sine_table


def unrotate(gradient, cosine_table, sine_table):
    half_size = gradient.shape[-1] // 2
    scaled = gradient * sine_table
    turned = jnp.concatenate([-scaled[..., half_size:], scaled[..., :half_size]], -1)
    return gradient * cosine_table - turned


def low_copy(tensor):
    rounded = lax.optimization_barrier(tensor.astype(jnp.bfloat16))
    return rounded.astype(jnp.float32)


def reference(inputs, queries, key_rows, values, out_grad, band_start, owners):
    block_rows = min(512, TOKENS)
    span_rows = block_rows + WINDOW
    query_heads = queries.astype(jnp.float32).reshape(TOKENS, KVH, QPK, HD)
    out_heads = out_grad.astype(jnp.float32).reshape(TOKENS, KVH, QPK, HD)
    front_zero = jnp.zeros((WINDOW, KVH, HD), jnp.float32)
    gathered_key_rows = jnp.concatenate([front_zero, key_rows.astype(jnp.float32).reshape(TOKENS, KVH, HD)], 0)
    value_all = jnp.concatenate([front_zero, values.astype(jnp.float32).reshape(TOKENS, KVH, HD)], 0)

    def one_block(totals, offset):
        grad_keys, grad_values = totals
        query_part = lax.dynamic_slice_in_dim(query_heads, offset, block_rows, 0)
        out_part = lax.dynamic_slice_in_dim(out_heads, offset, block_rows, 0)
        key_part = lax.dynamic_slice_in_dim(gathered_key_rows, offset, span_rows, 0)
        value_part = lax.dynamic_slice_in_dim(value_all, offset, span_rows, 0)
        band_part = lax.dynamic_slice_in_dim(band_start, offset, block_rows, 0)
        query_pos = offset + jnp.arange(block_rows, dtype=jnp.int32)
        key_pos = offset - WINDOW + jnp.arange(span_rows, dtype=jnp.int32)
        allowed = (key_pos[None, :] >= band_part[:, None]) & (key_pos[None, :] <= query_pos[:, None])
        attention_logits = jnp.einsum("qgrh,kgh->grqk", query_part, key_part, precision=top_precision) * score_scale
        masked = jnp.where(allowed, attention_logits, neg_large)
        row_top = jnp.max(masked, -1, keepdims=True)
        exponent = jnp.where(allowed, jnp.exp(masked - row_top), 0.0)
        attend = exponent / jnp.sum(exponent, -1, keepdims=True)
        attend_low = low_copy(attend)
        grad_attend = jnp.einsum("qgrh,kgh->grqk", out_part, value_part, precision=top_precision)
        row_dot = jnp.sum(attend * grad_attend, -1, keepdims=True)
        grad_score = low_copy(attend * (grad_attend - row_dot) * score_scale)
        query_term = jnp.einsum("grqk,kgh->qgrh", grad_score, key_part, precision=top_precision)
        key_term = jnp.einsum("grqk,qgrh->kgh", grad_score, query_part, precision=top_precision)
        value_term = jnp.einsum("grqk,qgrh->kgh", attend_low, out_part, precision=top_precision)
        grad_keys = lax.dynamic_update_slice_in_dim(
            grad_keys, lax.dynamic_slice_in_dim(grad_keys, offset, span_rows, 0) + key_term, offset, 0)
        grad_values = lax.dynamic_update_slice_in_dim(
            grad_values, lax.dynamic_slice_in_dim(grad_values, offset, span_rows, 0) + value_term, offset, 0)
        return (grad_keys, grad_values), query_term

    offsets = jnp.arange(TOKENS // block_rows, dtype=jnp.int32) * block_rows
    start_pair = (jnp.zeros((TOKENS + WINDOW, KVH, HD), jnp.float32),
                  jnp.zeros((TOKENS + WINDOW, KVH, HD), jnp.float32))
    (grad_keys, grad_values), query_blocks = lax.scan(one_block, start_pair, offsets)
    grad_query = query_blocks.reshape(TOKENS, KVH * QPK, HD)
    grad_keys = grad_keys[WINDOW:]
    grad_values = grad_values[WINDOW:]
    cosine_table, sine_table = rope_tables(jnp.arange(TOKENS, dtype=jnp.int32), HD)
    query_pre = unrotate(grad_query, cosine_table[:, None, :], sine_table[:, None, :])
    key_pre = unrotate(grad_keys, cosine_table[:, None, :], sine_table[:, None, :])
    column_grads = jnp.concatenate([
        query_pre.reshape(TOKENS, N_HEAD, KV_DEV * QPK * HD),
        key_pre.reshape(TOKENS, N_HEAD, KV_DEV * HD),
        grad_values.reshape(TOKENS, N_HEAD, KV_DEV * HD)], 2).reshape(TOKENS, N_HEAD * CPD).astype(jnp.bfloat16)

    shard_inputs = inputs.reshape(N_SEQ, TOK_DEV, D)
    shard_grads = column_grads.reshape(N_SEQ, TOK_DEV, N_HEAD * CPD)

    def add_shard(total, shard_pair):
        term = jnp.dot(shard_pair[0].T, shard_pair[1], preferred_element_type=jnp.float32)
        return total + low_copy(term), None

    summed, unused = lax.scan(add_shard, jnp.zeros((D, N_HEAD * CPD), jnp.float32), (shard_inputs, shard_grads))
    gradient = summed.astype(jnp.bfloat16)
    padded = jnp.pad(gradient, ((0, NBLK * BLOCK - D), (0, 0)))
    left_stat = jnp.zeros((N_SEQ, N_HEAD, BLOCK, BLOCK), jnp.float32)
    right_stat = jnp.zeros((N_SEQ, N_HEAD, CPD, CPD), jnp.float32)
    for group_index in range(N_HEAD):
        for block_index in range(NBLK):
            part_rows = padded[block_index * BLOCK:(block_index + 1) * BLOCK, group_index * CPD:(group_index + 1) * CPD]
            holder = owners[group_index, block_index]
            left_value = jnp.dot(part_rows, part_rows.T, preferred_element_type=jnp.float32) / TOKENS
            right_value = jnp.dot(part_rows.T, part_rows, preferred_element_type=jnp.float32) / TOKENS
            left_stat = left_stat.at[holder, group_index].set(left_value)
            right_stat = right_stat.at[holder, group_index].set(right_value)
    return (left_stat, right_stat)
```

```python
import functools

import jax
import jax.numpy as jnp
from jax import lax
from jax.experimental import pallas as pl
from jax.experimental.pallas import tpu as pltpu
from jax.sharding import PartitionSpec as P

D = 5376
HD = 128
KV_DEV = 2
QPK = 2
WINDOW = 1024
BLOCK = 1024
NBLK = 6


score_scale = 168.0 ** (-0.5)
log2_e = 1.4426950408889634
rotary_frequency_base = 10000.0
neg_large = -1e30


CHUNK = 128
CHUNKS = BLOCK // CHUNK
MESH = pl.DeviceIdType.MESH


def rope_tables(positions, head_size):
    half_size = head_size // 2
    frequency = jnp.power(
        rotary_frequency_base, -2.0 * jnp.arange(half_size, dtype=jnp.float32) / head_size
    )
    angles = frequency[:, None] * positions.astype(jnp.float32)[None, :]
    return (jnp.cos(angles), jnp.sin(angles))


def unrotate(gradient, cosine, sine):
    first, second = gradient[: HD // 2], gradient[HD // 2 :]
    return jnp.concatenate([first * cosine + second * sine, second * cosine - first * sine], 0)


def dot(left, right, left_dim, right_dim):
    return lax.dot_general(
        left, right, (((left_dim,), (right_dim,)), ((), ())), preferred_element_type=jnp.float32
    )


def layer_kernel(
    sizes,
    pick_ref,
    band_ref,
    cos_ref,
    sin_ref,
    inputs_ref,
    query_ref,
    out_ref,
    key_ref,
    value_ref,
    block_ref,
    layer,
    grads,
    keys,
    vals,
    rim_out,
    rim_in,
    totals,
    pieces,
    pair_out,
    pair_in,
    kept,
    chip_out,
    chip_in,
    kv_send,
    kv_recv,
    rim_send,
    rim_recv,
    up_send,
    up_recv,
    down_send,
    down_recv,
    pair_send,
    pair_recv,
    chip_send,
    chip_recv,
):
    tok_rows, seq_count, head_count = sizes
    part_rows = tok_rows // head_count
    chips = seq_count // 2
    hops = head_count - 1
    block_rows = min(256, tok_rows)
    span_rows = block_rows + WINDOW
    seq = lax.axis_index("seq")
    group = lax.axis_index("head")
    core = lax.rem(seq, 2)
    chip = lax.div(seq, 2)
    sibling = seq + 1 - 2 * core
    beside = seq - 1 + 2 * core
    has_beside = (beside >= 0) & (beside < seq_count)
    has_above = group + 1 < head_count
    has_below = group >= 1
    has_next = seq + 1 < seq_count
    has_previous = seq >= 1

    barrier = pltpu.get_barrier_semaphore()

    def greet(seq_at, group_at):
        pl.semaphore_signal(barrier, inc=1, device_id=(seq_at, group_at), device_id_type=MESH)

    def other_chip(d):
        return 2 * lax.rem(chip + d, chips) + core

    greet(sibling, group)
    for d in range(1, chips):
        greet(other_chip(d), group)
    for condition, seq_at, group_at in (
        (has_beside, beside, group),
        (has_above, seq, group + 1),
        (has_below, seq, group - 1),
    ):
        pl.when(condition)(functools.partial(greet, seq_at, group_at))
    peers = chips + sum(
        jnp.where(condition, 1, 0) for condition in (has_beside, has_above, has_below)
    )
    pl.semaphore_wait(barrier, peers)

    def remote(source, target, send, recv, seq_at, group_at):
        return pltpu.make_async_remote_copy(
            src_ref=source,
            dst_ref=target,
            send_sem=send,
            recv_sem=recv,
            device_id=(seq_at, group_at),
            device_id_type=MESH,
        )

    def kv_copy(i, source, joined):
        target = joined.at[pl.ds(0, tok_rows)]
        return remote(source, target, kv_send.at[i], kv_recv.at[i], seq + 1, group)

    @pl.when(has_next)
    def _():
        kv_copy(0, key_ref, keys).start()
        kv_copy(1, value_ref, vals).start()

    widths = [
        CHUNK * sum(b * BLOCK + c * CHUNK < D for b in range(NBLK)) for c in range(CHUNKS)
    ]

    def shard_rows(shard):
        return pl.ds(pl.multiple_of(shard * part_rows, part_rows), part_rows)

    def layer_part(c, shard):
        return layer.at[c, shard_rows(shard), pl.ds(0, widths[c])]

    def up_copy(k, c, shard):
        part = layer_part(c, shard)
        return remote(part, part, up_send.at[k, c], up_recv.at[k, c], seq, group + 1)

    def down_copy(k, c, shard):
        part = layer_part(c, shard)
        return remote(part, part, down_send.at[k, c], down_recv.at[k, c], seq, group - 1)

    def arrive(k, c):
        @pl.when(group - 1 - k >= 0)
        def _():
            up_copy(k, c, group - 1 - k).wait_recv()

        @pl.when(group + 1 + k < head_count)
        def _():
            down_copy(k, c, group + 1 + k).wait_recv()

    def sends(k):
        return (
            ((group - k >= 0) & has_above, up_copy, group - k),
            ((group + k < head_count) & has_below, down_copy, group + k),
        )

    def issue(k, c):
        if k > 0:
            arrive(k - 1, c)
        for condition, make, shard in sends(k):

            @pl.when(condition)
            def _(make=make, shard=shard):
                make(k, c, shard).start()

    def ahead(k):
        return min(CHUNKS, 2 * (hops - k))

    for c in range(CHUNKS):
        for b in range(widths[c] // CHUNK):
            low = b * BLOCK + c * CHUNK
            layer[c, shard_rows(group), b * CHUNK : (b + 1) * CHUNK] = inputs_ref[
                :, low : low + CHUNK
            ]
        if c < ahead(0):
            issue(0, c)

    keys[tok_rows:] = key_ref[...]
    vals[tok_rows:] = value_ref[...]

    @pl.when(has_previous)
    def _():
        kv_copy(0, key_ref, keys).wait_recv()
        kv_copy(1, value_ref, vals).wait_recv()

    @pl.when(jnp.logical_not(has_previous))
    def _():
        keys[:tok_rows] = jnp.zeros((tok_rows, KV_DEV * HD), jnp.bfloat16)
        vals[:tok_rows] = jnp.zeros((tok_rows, KV_DEV * HD), jnp.bfloat16)

    def rim_copy(g):
        return remote(
            rim_out.at[g], rim_in.at[g], rim_send.at[g], rim_recv.at[g], seq - 1, group
        )

    own = lax.broadcasted_iota(jnp.int32, (1, block_rows), 1) + WINDOW
    own = jnp.concatenate([own] * QPK, 1)

    for g in range(KV_DEV):
        lanes = slice(g * HD, (g + 1) * HD)
        totals[g] = jnp.zeros((2, 2 * tok_rows, HD), jnp.float32)

        @pl.loop(0, tok_rows // block_rows)
        def _(step, g=g, lanes=lanes):
            offset = pl.multiple_of(step * block_rows, block_rows)
            rows = pl.ds(offset, block_rows)
            span = pl.ds(pl.multiple_of(tok_rows - WINDOW + offset, 128), span_rows)
            key_part = keys[span, lanes]
            value_part = vals[span, lanes]
            heads = [slice(q * HD, (q + 1) * HD) for q in range(g * QPK, (g + 1) * QPK)]
            query_part = jnp.concatenate([query_ref[rows, head] for head in heads], 0)
            out_part = jnp.concatenate([out_ref[rows, head] for head in heads], 0)
            band = band_ref[:, rows] - (offset - WINDOW)
            band = jnp.concatenate([band] * QPK, 1)
            key_at = lax.broadcasted_iota(jnp.int32, (span_rows, QPK * block_rows), 0)

            scores = dot(key_part, query_part, 1, 1)
            scores = jnp.where((key_at >= band) & (key_at <= own), scores, neg_large)
            row_top = jnp.max(scores, 0, keepdims=True)
            exponent = jnp.exp2((scores - row_top) * (score_scale * log2_e))
            inverse = 1.0 / jnp.sum(exponent, 0, keepdims=True)
            grad_attend = dot(value_part, out_part, 1, 1)
            attend = exponent * inverse
            row_dot = jnp.sum(attend * grad_attend, 0, keepdims=True)
            attend_low = attend.astype(jnp.bfloat16)
            grad_score = (attend * (grad_attend - row_dot) * score_scale).astype(jnp.bfloat16)
            totals[g, 0, span, :] += dot(grad_score, query_part, 1, 0)
            totals[g, 1, span, :] += dot(attend_low, out_part, 1, 0)
            grad_query = dot(key_part, grad_score, 0, 0)
            cosine = cos_ref[:, rows]
            sine = sin_ref[:, rows]
            for r, head in enumerate(heads):
                part = grad_query[:, r * block_rows : (r + 1) * block_rows]
                grads[head, rows] = unrotate(part, cosine, sine).astype(jnp.bfloat16)

        rim_out[g] = totals[g, :, :tok_rows].astype(jnp.bfloat16)

        @pl.when(has_previous)
        def _(g=g):
            rim_copy(g).start()

        if g < KV_DEV - 1:
            for k in range(1, min(2, hops)):
                for c in range(2):
                    issue(k, c)

    for k in range(1, hops):
        for c in range(2 if k == 1 else 0, ahead(k)):
            issue(k, c)

    for g in range(KV_DEV):

        @pl.when(has_next)
        def _(g=g):
            rim_copy(g).wait_recv()

        @pl.when(jnp.logical_not(has_next))
        def _(g=g):
            rim_in[g] = jnp.zeros((2, tok_rows, HD), jnp.bfloat16)

        grad_key = totals[g, 0, tok_rows:] + rim_in[g, 0].astype(jnp.float32)
        grad_value = totals[g, 1, tok_rows:] + rim_in[g, 1].astype(jnp.float32)
        first = (KV_DEV * QPK + g) * HD
        grads[first : first + HD, :] = unrotate(grad_key.T, cos_ref[...], sin_ref[...]).astype(
            jnp.bfloat16
        )
        first += KV_DEV * HD
        grads[first : first + HD, :] = grad_value.T.astype(jnp.bfloat16)

    pieces[...] = jnp.zeros(pieces.shape, jnp.bfloat16)

    def pair_copy(slot):
        return remote(
            pair_out.at[slot], pair_in.at[slot], pair_send.at[slot], pair_recv.at[slot], sibling, group
        )

    def chip_copy(slot, d):
        return remote(
            chip_out.at[slot, d - 1],
            chip_in.at[slot, d - 1],
            chip_send.at[slot, d - 1],
            chip_recv.at[slot, d - 1],
            other_chip(d),
            group,
        )

    def finish(c):
        slot = c % 2
        total = kept[slot].astype(jnp.float32)
        for d in range(1, chips):
            chip_copy(slot, d).wait()
            total += chip_in[slot, d - 1].astype(jnp.float32)
        block_ref[:, c * CHUNK : (c + 1) * CHUNK] = total.astype(jnp.bfloat16)

    for c in range(CHUNKS):
        slot = c % 2
        for k in range(hops - 1, -1, -1):
            if ahead(k) <= c + 2 * (hops - k) < CHUNKS:
                issue(k, c + 2 * (hops - k))
        arrive(hops - 1, c)
        if c > 0 and widths[c] < widths[c - 1]:
            for b in range(widths[c] // CHUNK, widths[c - 1] // CHUNK):
                pieces[b] = jnp.zeros((pieces.shape[1], CHUNK), jnp.bfloat16)
        product = dot(grads[...], layer[c, :, : widths[c]], 1, 0).astype(jnp.bfloat16)
        for b in range(widths[c] // CHUNK):
            pieces[b] = product[:, b * CHUNK : (b + 1) * CHUNK]
        for j in range(chips):
            pair_out[slot, j] = pieces[pick_ref[2 * j + 1 - core]]
        pair_copy(slot).start()
        pair_copy(slot).wait()
        if c > 0:
            finish(c - 1)
        kept[slot] = (
            pieces[pick_ref[2 * chip + core]].astype(jnp.float32)
            + pair_in[slot, chip].astype(jnp.float32)
        ).astype(jnp.bfloat16)
        for d in range(1, chips):
            at = lax.rem(chip + d, chips)
            chip_out[slot, d - 1] = (
                pieces[pick_ref[2 * at + core]].astype(jnp.float32)
                + pair_in[slot, at].astype(jnp.float32)
            ).astype(jnp.bfloat16)
            chip_copy(slot, d).start()
    finish(CHUNKS - 1)

    @pl.when(has_next)
    def _():
        kv_copy(0, key_ref, keys).wait_send()
        kv_copy(1, value_ref, vals).wait_send()

    @pl.when(has_previous)
    def _():
        for g in range(KV_DEV):
            rim_copy(g).wait_send()

    for k in range(hops):
        for condition, make, shard in sends(k):

            @pl.when(condition)
            def _(make=make, shard=shard, k=k):
                for c in range(CHUNKS):
                    make(k, c, shard).wait_send()


def owned_block(pick, band, cosine, sine, inputs, queries, out_grad, key_rows, values):
    tok_rows = queries.shape[0]
    seq_count = lax.axis_size("seq")
    head_count = lax.axis_size("head")
    chips = seq_count // 2
    hops = head_count - 1
    columns = KV_DEV * (QPK + 2) * HD
    low = jnp.bfloat16
    dma = pltpu.SemaphoreType.DMA
    vmem = pl.BlockSpec(memory_space=pltpu.VMEM)
    return pl.pallas_call(
        functools.partial(layer_kernel, (tok_rows, seq_count, head_count)),
        in_specs=[pl.BlockSpec(memory_space=pltpu.SMEM)] + [vmem] * 8,
        out_specs=vmem,
        out_shape=jax.ShapeDtypeStruct((columns, BLOCK), low),
        scratch_shapes=[
            pltpu.VMEM((CHUNKS, tok_rows, NBLK * CHUNK), low),
            pltpu.VMEM((columns, tok_rows), low),
            pltpu.VMEM((2 * tok_rows, KV_DEV * HD), low),
            pltpu.VMEM((2 * tok_rows, KV_DEV * HD), low),
            pltpu.VMEM((KV_DEV, 2, tok_rows, HD), low),
            pltpu.VMEM((KV_DEV, 2, tok_rows, HD), low),
            pltpu.VMEM((KV_DEV, 2, 2 * tok_rows, HD), jnp.float32),
            pltpu.VMEM((NBLK + 1, columns, CHUNK), low),
            pltpu.VMEM((2, chips, columns, CHUNK), low),
            pltpu.VMEM((2, chips, columns, CHUNK), low),
            pltpu.VMEM((2, columns, CHUNK), low),
            pltpu.VMEM((2, chips - 1, columns, CHUNK), low),
            pltpu.VMEM((2, chips - 1, columns, CHUNK), low),
            dma((2,)),
            dma((2,)),
            dma((KV_DEV,)),
            dma((KV_DEV,)),
            dma((hops, CHUNKS)),
            dma((hops, CHUNKS)),
            dma((hops, CHUNKS)),
            dma((hops, CHUNKS)),
            dma((2,)),
            dma((2,)),
            dma((2, chips - 1)),
            dma((2, chips - 1)),
        ],
        compiler_params=pltpu.CompilerParams(
            collective_id=0, has_side_effects=True, vmem_limit_bytes=60 * 2**20
        ),
        name="owned_block",
    )(pick, band, cosine, sine, inputs, queries, out_grad, key_rows, values)


def per_device(inputs, queries, key_rows, values, out_grad, band_start, owners):
    tok_rows = queries.shape[0]
    seq_count = lax.axis_size("seq")
    seq_index = lax.axis_index("seq")
    group_index = lax.axis_index("head")
    tokens_all = tok_rows * seq_count
    positions = seq_index * tok_rows + jnp.arange(tok_rows, dtype=jnp.int32)
    cosine, sine = rope_tables(positions, HD)
    owner_row = lax.dynamic_index_in_dim(owners, group_index, 0, keepdims=False)
    held = owner_row[None, :] == jnp.arange(seq_count, dtype=jnp.int32)[:, None]
    order = jnp.arange(NBLK, dtype=jnp.int32)[None, :]
    pick = NBLK + jnp.sum(jnp.where(held, order - NBLK, 0), 1, dtype=jnp.int32)
    band = (band_start - seq_index * tok_rows)[None, :]
    block = owned_block(
        pick, band, cosine, sine, inputs, queries, out_grad, key_rows, values
    )
    left_stat = dot(block, block, 0, 0) / tokens_all
    right_stat = dot(block, block, 1, 1) / tokens_all
    return (left_stat[None, None], right_stat[None, None])


def solution(mesh):
    in_specs = (
        P(("seq", "head"), None),
        P("seq", "head"),
        P("seq", "head"),
        P("seq", "head"),
        P("seq", "head"),
        P("seq"),
        P(),
    )
    out_specs = (P("seq", "head", None, None), P("seq", "head", None, None))
    return jax.shard_map(
        per_device, mesh=mesh, in_specs=in_specs, out_specs=out_specs, check_vma=False
    )
```
